128 devices in a mesh: dp: 16 (over y, x), tensor: 8 (over z, core).
Axes of the slice: x: 4, y: 4, z: 4, core: 2. Of those that a mesh axis runs over, the one named last changes fastest.
Arguments:
- tokens: bfloat16 [4096, 7168], P('dp', 'tensor'), may hold values from -6 to 6
- cotangent: bfloat16 [4096, 7168], P('dp', 'tensor'), may hold values from -4 to 4
- up_weight: bfloat16 [112, 1792, 128], P('tensor', 'dp'), may hold values from -0.125 to 0.125
- down_weight: bfloat16 [112, 1792, 128], P('tensor', 'dp'), may hold values from -0.09375 to 0.09375
- up_kept: int32 [112, 14], P('tensor'), may hold values from 0 to 55, as said below
- down_kept: int32 [112, 14], P('tensor'), may hold values from 0 to 55, as said below
Outputs:
- output: bfloat16 [4096, 7168], P('dp', 'tensor')
- input_grad: bfloat16 [4096, 7168], P('dp', 'tensor')
- up_grad: bfloat16 [112, 1792, 128], P('tensor', 'dp')
- down_grad: bfloat16 [112, 1792, 128], P('tensor', 'dp')
The draws below stay inside these ranges and needn't reach their ends.
Inputs may be any that keep to these rules, and one draw needn't show every extreme that they name: `up_kept`: each row names 14 different feature blocks; every feature block is named by some row. `down_kept`: each row names 14 different feature blocks; every feature block is named by some row.
All inputs are finite; a program needn't handle non-finite values.
Results may differ from the reference program's by a relative error of at most 0.018.
Values may be sent and summed in bfloat16 or wider, within the bound.
No kernel may reach another device: no remote copies, remote signals or barrier semaphores. Data moves between devices by JAX's collectives and lax.ppermute only.
A program may use at most 192 MiB of HBM per device.

```python
import jax
import jax.numpy as jnp
from jax import lax

D = 7168
FF = 14336
BLK = 128
TOK_DEV = 256
KEEP = 14
NBF = 112
TOKENS = 4096
N_DP = 16
N_TENSOR = 8


def kept_blocks(key):
    block_count = D // BLK
    first_key, second_key = jax.random.split(key)
    starts = jax.random.permutation(first_key, NBF).astype(jnp.int32)
    row_keys = jax.random.split(second_key, NBF)

    def row_offsets(subkey):
        return jax.random.permutation(subkey, block_count - 1).astype(jnp.int32)
    offsets = jax.vmap(row_offsets)(row_keys)
    chosen = jnp.concatenate([jnp.zeros((NBF, 1), jnp.int32), offsets[:, :KEEP - 1] + 1], axis=1)
    return ((starts[:, None] + chosen) % block_count).astype(jnp.int32)


def draw_up_kept(key, part):
    key = jax.random.fold_in(key, 11)
    return kept_blocks(key)


def draw_down_kept(key, part):
    key = jax.random.fold_in(key, 23)
    return kept_blocks(key)


def shard_levels(stream_key, shape, cuts, smallest, high):
    factor_of = 1.0
    for position, parts in cuts:
        heights = jax.random.uniform(jax.random.fold_in(jax.random.fold_in(stream_key, 6), position), (parts,), jnp.float32, smallest / len(cuts), high / len(cuts))
        factor_of = factor_of * jnp.repeat(jnp.exp(heights), shape[position] // parts).reshape((-1,) + (1,) * (len(shape) - 1 - position))
    return factor_of


def bell_draw(rng, extent, deviation, bound, cuts=(), held_as=jnp.bfloat16):
    array = jax.random.normal(rng, extent, jnp.float32) * deviation
    if len(cuts) > 0:
        array = shard_levels(rng, extent, cuts, -0.22, 0.18) * array
    return jnp.clip(array, min=-bound, max=bound).astype(held_as)


def setup_inputs(seed: int = 0) -> dict:
    splits = jax.random.split(jax.random.key(seed), 7)
    return {
        "tokens": bell_draw(splits[0], (TOKENS, D), 1.0, 6.0, ((0, 16), (1, 8))),
        "cotangent": bell_draw(splits[1], (TOKENS, D), 0.25, 4.0, ((0, 16), (1, 8))),
        "up_weight": bell_draw(splits[2], (NBF, KEEP * BLK, BLK), (KEEP * BLK) ** -0.5, 0.125, ((0, 8), (1, 16))),
        "down_weight": bell_draw(splits[3], (NBF, KEEP * BLK, BLK), (FF // 4) ** -0.5, 0.09375, ((0, 8), (1, 16))),
        "up_kept": draw_up_kept(jax.random.fold_in(splits[6], 71), 0),
        "down_kept": draw_down_kept(jax.random.fold_in(splits[6], 71), 0),
    }


def gelu_tanh(value):
    return jax.nn.gelu(value, approximate=True)

def shard_terms(tok_blocks, cot_blocks, up_local, down_local, up_index, down_index):
    token_count = tok_blocks.shape[0]
    local_count = up_local.shape[0]
    gathered = tok_blocks[:, up_index.reshape(-1)].reshape(token_count, local_count, KEEP * BLK)
    pre_act = jnp.einsum('tfr,fre->tfe', gathered.astype(jnp.float32), up_local.astype(jnp.float32))
    hidden = gelu_tanh(pre_act).astype(jnp.bfloat16)
    down_four = down_local.reshape(local_count, KEEP, BLK, BLK)
    out_terms = jnp.einsum('tfe,fked->tfkd', hidden.astype(jnp.float32), down_four.astype(jnp.float32))
    out_part = jnp.zeros((token_count, D // BLK, BLK), jnp.float32)
    out_part = out_part.at[:, down_index.reshape(-1)].add(out_terms.reshape(token_count, local_count * KEEP, BLK))
    cot_gathered = cot_blocks[:, down_index.reshape(-1)].reshape(token_count, local_count, KEEP, BLK)
    grad_hidden = jnp.einsum('tfkd,fked->tfe', cot_gathered.astype(jnp.float32), down_four.astype(jnp.float32))
    unused, gelu_pull = jax.vjp(gelu_tanh, pre_act)
    grad_pre = gelu_pull(grad_hidden)[0].astype(jnp.bfloat16)
    down_term = jnp.einsum('tfe,tfkd->fked', hidden.astype(jnp.float32), cot_gathered.astype(jnp.float32))
    up_term = jnp.einsum('tfr,tfe->fre', gathered.astype(jnp.float32), grad_pre.astype(jnp.float32))
    up_four = up_local.reshape(local_count, KEEP, BLK, BLK)
    input_terms = jnp.einsum('tfe,fkce->tfkc', grad_pre.astype(jnp.float32), up_four.astype(jnp.float32))
    input_part = jnp.zeros((token_count, D // BLK, BLK), jnp.float32)
    input_part = input_part.at[:, up_index.reshape(-1)].add(input_terms.reshape(token_count, local_count * KEEP, BLK))
    return (out_part, input_part, up_term, down_term.reshape(local_count, KEEP * BLK, BLK))

def round_trip(value):
    return lax.optimization_barrier(value.astype(jnp.bfloat16)).astype(jnp.float32)

def reference(tokens, cotangent, up_weight, down_weight, up_kept, down_kept):
    local_count = NBF // N_TENSOR
    tok_groups = tokens.reshape(N_DP, TOK_DEV, D // BLK, BLK)
    cot_groups = cotangent.reshape(N_DP, TOK_DEV, D // BLK, BLK)
    up_split = up_weight.reshape(N_TENSOR, local_count, KEEP * BLK, BLK)
    down_split = down_weight.reshape(N_TENSOR, local_count, KEEP * BLK, BLK)
    up_index = up_kept.reshape(N_TENSOR, local_count, KEEP)
    down_index = down_kept.reshape(N_TENSOR, local_count, KEEP)

    def one_group(carry, inputs):
        tok_blocks, cot_blocks = inputs

        def one_shard(pieces):
            return shard_terms(tok_blocks, cot_blocks, pieces[0], pieces[1], pieces[2], pieces[3])
        out_parts, input_parts, up_terms, down_terms = lax.map(one_shard, (up_split, down_split, up_index, down_index))
        output = lax.optimization_barrier(jnp.sum(round_trip(out_parts), axis=0)).astype(jnp.bfloat16)
        input_grad = lax.optimization_barrier(jnp.sum(round_trip(input_parts), axis=0)).astype(jnp.bfloat16)
        new_carry = (carry[0] + round_trip(up_terms), carry[1] + round_trip(down_terms))
        return (new_carry, (output.reshape(TOK_DEV, D), input_grad.reshape(TOK_DEV, D)))
    start = (jnp.zeros((N_TENSOR, local_count, KEEP * BLK, BLK), jnp.float32), jnp.zeros((N_TENSOR, local_count, KEEP * BLK, BLK), jnp.float32))
    sums, results = lax.scan(one_group, start, (tok_groups, cot_groups))
    output = results[0].reshape(TOKENS, D)
    input_grad = results[1].reshape(TOKENS, D)
    up_grad = sums[0].reshape(NBF, KEEP * BLK, BLK).astype(jnp.bfloat16)
    down_grad = sums[1].reshape(NBF, KEEP * BLK, BLK).astype(jnp.bfloat16)
    return (output, input_grad, up_grad, down_grad)
```

```python
import functools

import jax
import jax.numpy as jnp
from jax import lax
from jax.experimental import pallas as pl
from jax.experimental.pallas import tpu as pltpu
from jax.sharding import PartitionSpec as P

D = 7168
BLK = 128
KEEP = 14
NFB = D // BLK
ROWS = KEEP * BLK
F32 = jnp.float32
BF16 = jnp.bfloat16
SIDE = 4
STEP = (0, -1, 1, 2)


def gelu_and_slope(v):
    c = 0.7978845608028654
    v2 = v * v
    th = jnp.tanh(c * (v + 0.044715 * v * v2))
    half = 0.5 * (1.0 + th)
    slope = half + 0.5 * v * (1.0 - th * th) * (c * (1.0 + 3 * 0.044715 * v2))
    return v * half, slope


def layer_kernel(
    has_prev, local, rows_tbl, upk, dnk, tok, cot,
    u0, um, up, u2a, u2b, d0, dm, dp, d2a, d2b, *rest
):
    if has_prev:
        prev_out, prev_in = rest[:2]
        rest = rest[2:]
    (out_ref, in_ref,
     tu0, tum, tup, tu2a, tu2b, td0, tdm, tdp, td2a, td2b,
     tokg, cotg, upw, dnw, dnr, uterm, dterm, out_acc, in_acc) = rest
    j = pl.program_id(0)

    @pl.when(j == 0)
    def _():
        out_acc[...] = jnp.zeros_like(out_acc)
        in_acc[...] = jnp.zeros_like(in_acc)

    part = u0.shape[2]

    def pieces(group):
        g0, gm, gp, g2a, g2b = group
        for g, ref in enumerate((g0, gm, gp)):
            for s in range(4):
                yield g * 4 + s, ref, s
        for s in range(4):
            yield 12 + s, (g2a if s < 2 else g2b), s % 2

    def at(which, i):
        return pl.ds(pl.multiple_of(rows_tbl[which, i], 16), part)

    for i, ref, s in pieces((u0, um, up, u2a, u2b)):
        upw[at(0, i), :] = ref[s, 0]
    for i, ref, s in pieces((d0, dm, dp, d2a, d2b)):
        dnr[at(1, i), :] = ref[s, 0]
    for k in range(KEEP):
        cols = slice(k * BLK, (k + 1) * BLK)
        tokg[:, cols] = tok[upk[j, k]]
        cotg[:, cols] = cot[dnk[j, k]]
        dnw[:, cols] = dnr[cols, :]

    pre = jnp.dot(tokg[...], upw[...], preferred_element_type=F32)
    nt = (((1,), (1,)), ((), ()))
    tn = (((0,), (0,)), ((), ()))
    grad_hidden = lax.dot_general(cotg[...], dnw[...], nt, preferred_element_type=F32)
    hid, slope = gelu_and_slope(pre)
    hidden = hid.astype(BF16)
    grad_pre = (grad_hidden * slope).astype(BF16)

    dt = lax.dot_general(hidden, cotg[...], tn, preferred_element_type=F32).astype(BF16)
    ut = lax.dot_general(tokg[...], grad_pre, tn, preferred_element_type=F32).astype(BF16)
    uterm[...] = ut
    for k in range(KEEP):
        cols = slice(k * BLK, (k + 1) * BLK)
        dterm[cols, :] = dt[:, cols]
    for k in range(KEEP):
        cols = slice(k * BLK, (k + 1) * BLK)
        out_acc[dnk[j, k]] += jnp.dot(hidden, dnw[:, cols], preferred_element_type=F32)
        in_acc[upk[j, k]] += lax.dot_general(
            grad_pre, upw[cols, :], nt, preferred_element_type=F32
        )
    for i, ref, s in pieces((tu0, tum, tup, tu2a, tu2b)):
        ref[s, 0] = uterm[at(0, i), :]
    for i, ref, s in pieces((td0, tdm, tdp, td2a, td2b)):
        ref[s, 0] = dterm[at(1, i), :]

    @pl.when(j == local - 1)
    def _():
        def put(f, carry):
            a, b = out_acc[f], in_acc[f]
            if has_prev:
                a = a + prev_out[f].astype(F32)
                b = b + prev_in[f].astype(F32)
            out_ref[f] = a.astype(BF16)
            in_ref[f] = b.astype(BF16)
            return carry

        lax.fori_loop(0, NFB, put, 0)


def layer_part(rows_tbl, upk, dnk, tok, cot, up_group, dn_group, prev):
    local, part = up_group[0].shape[1:3]
    tokens = tok.shape[1]
    whole = pl.BlockSpec((NFB, tokens, BLK), lambda j, *_: (0, 0, 0), pipeline_mode=pl.Buffered(1))

    def piece(n):
        return pl.BlockSpec((n, 1, part, BLK), lambda j, *_: (0, j, 0, 0))

    def shape(n):
        return jax.ShapeDtypeStruct((n, local, part, BLK), BF16)

    five = (4, 4, 4, 2, 2)
    sums = jax.ShapeDtypeStruct((NFB, tokens, BLK), BF16)
    outs = pl.pallas_call(
        functools.partial(layer_kernel, prev is not None, local),
        grid_spec=pltpu.PrefetchScalarGridSpec(
            num_scalar_prefetch=3,
            grid=(local,),
            in_specs=[whole, whole] + [piece(n) for n in five + five]
            + ([whole, whole] if prev is not None else []),
            out_specs=[whole, whole] + [piece(n) for n in five + five],
            scratch_shapes=[
                pltpu.VMEM((tokens, ROWS), BF16),
                pltpu.VMEM((tokens, ROWS), BF16),
                pltpu.VMEM((ROWS, BLK), BF16),
                pltpu.VMEM((BLK, ROWS), BF16),
                pltpu.VMEM((ROWS, BLK), BF16),
                pltpu.VMEM((ROWS, BLK), BF16),
                pltpu.VMEM((ROWS, BLK), BF16),
                pltpu.VMEM((NFB, tokens, BLK), F32),
                pltpu.VMEM((NFB, tokens, BLK), F32),
            ],
        ),
        out_shape=[sums, sums] + [shape(n) for n in five + five],
        compiler_params=pltpu.CompilerParams(vmem_limit_bytes=52 * 2**20),
        cost_estimate=pl.CostEstimate(
            flops=local * 12 * tokens * ROWS * BLK,
            bytes_accessed=4 * NFB * tokens * BLK * 2 + 8 * local * ROWS * BLK,
            transcendentals=local * tokens * BLK,
        ),
    )(rows_tbl, upk, dnk, tok, cot, *up_group, *dn_group, *(prev or ()))
    return outs[:2], outs[2:7], outs[7:]


def shift_perm(dx, dy):
    return [
        (y * SIDE + x, ((y + dy) % SIDE) * SIDE + (x + dx) % SIDE)
        for y in range(SIDE) for x in range(SIDE)
    ]


def shift(value, axis, by):
    return lax.ppermute(value, "dp", shift_perm(by, 0) if axis == 0 else shift_perm(0, by))


def gather_first(shard, axis):
    return jnp.stack(
        [shard, shift(shard, axis, 1), shift(shard, axis, -1), shift(shard, axis, 2)]
    )


def gather_second(group, axis):
    from_minus, from_plus = shift(group, axis, 1), shift(group, axis, -1)
    return (group, from_minus, from_plus,
            shift(from_minus[:2], axis, 1), shift(from_plus[2:], axis, -1))


def add(*terms):
    return sum(t.astype(F32) for t in terms).astype(BF16)


def reduce_first(terms, axis):
    own, to_minus, to_plus, far_a, far_b = terms
    got_a, got_b = shift(far_a, axis, 1), shift(far_b, axis, -1)
    send_plus = jnp.concatenate([add(to_plus[:2], got_a), to_plus[2:]])
    send_minus = jnp.concatenate([to_minus[:2], add(to_minus[2:], got_b)])
    return own, shift(send_plus, axis, 1), shift(send_minus, axis, -1)


def reduce_second(parts, axis):
    slot = [add(*(p[s] for p in parts)) for s in range(4)]
    return add(slot[0], shift(slot[1], axis, -1), shift(slot[2], axis, 1), shift(slot[3], axis, 2))


CHUNKS = 2


def body(tokens, cotangent, up_weight, down_weight, up_kept, down_kept):
    count, part = up_weight.shape[:2]
    per = count // CHUNKS
    rows = tokens.shape[0]

    def blocks(a):
        return a.reshape(rows, -1, BLK).transpose(1, 0, 2)

    tok = lax.all_gather(blocks(tokens), "tensor", axis=0, tiled=True)
    cot = lax.all_gather(blocks(cotangent), "tensor", axis=0, tiled=True)

    me = lax.axis_index("dp")
    y, x = me // SIDE, me % SIDE
    far = jnp.array(STEP, jnp.int32)
    ys, xs = (y + far) % SIDE, (x + far) % SIDE
    up_tbl = (ys[:, None] * SIDE + xs[None, :]).reshape(-1)
    dn_tbl = (ys[None, :] * SIDE + xs[:, None]).reshape(-1)
    rows_tbl = jnp.stack([up_tbl, dn_tbl]) * part

    groups = []
    for c in range(CHUNKS):
        own = slice(c * per, (c + 1) * per)
        u, d = gather_first(up_weight[own], 0), gather_first(down_weight[own], 1)
        groups.append((gather_second(u, 1), gather_second(d, 0)))
    sums, grads = None, []
    for c, (u, d) in enumerate(groups):
        own = slice(c * per, (c + 1) * per)
        sums, ut, dt = layer_part(rows_tbl, up_kept[own], down_kept[own], tok, cot, u, d, sums)
        grads.append((ut, dt))

    outs = [
        lax.psum_scatter(s, "tensor", scatter_dimension=0, tiled=True)
        .transpose(1, 0, 2).reshape(rows, -1)
        for s in sums
    ]
    ups, dns = [], []
    for ut, dt in grads:
        u, d = reduce_first(ut, 1), reduce_first(dt, 0)
        ups.append(reduce_second(u, 0))
        dns.append(reduce_second(d, 1))
    return outs[0], outs[1], jnp.concatenate(ups), jnp.concatenate(dns)


def solution(mesh):
    placed = (
        P("dp", "tensor"),
        P("dp", "tensor"),
        P("tensor", "dp", None),
        P("tensor", "dp", None),
        P("tensor", None),
        P("tensor", None),
    )
    return jax.shard_map(
        body,
        mesh=mesh,
        in_specs=placed,
        out_specs=placed[:4],
        check_vma=False,
    )
```

```python
import functools

import jax
import jax.numpy as jnp
from jax import lax
from jax.experimental import pallas as pl
from jax.experimental.pallas import tpu as pltpu
from jax.sharding import PartitionSpec as P

D = 7168
BLK = 128
KEEP = 14
NFB = D // BLK
ROWS = KEEP * BLK
F32 = jnp.float32
BF16 = jnp.bfloat16
SIDE = 4
STEP = (0, -1, 1, 2)
TENSOR = 8
VMEM_LIMIT = 56 * 2**20
MANY = 2
NT = (((1,), (1,)), ((), ()))
TN = (((0,), (0,)), ((), ()))


def gelu_and_slope(v):
    c = 0.7978845608028654
    v2 = v * v
    th = jnp.tanh(c * (v + 0.044715 * v * v2))
    half = 0.5 * (1.0 + th)
    slope = half + 0.5 * v * (1.0 - th * th) * (c * (1.0 + 3 * 0.044715 * v2))
    return v * half, slope


def cols(k):
    return slice(k * BLK, (k + 1) * BLK)


def pieces(rows_tbl, halves):
    for n, ref in enumerate(halves):
        for s in range(2):
            yield pl.ds(pl.multiple_of(rows_tbl[n * 2 + s], 16), ref.shape[3]), ref, s


def layer_kernel(base, has_prev, rows_tbl, upk, dnk, acts, *rest):
    w_in, rest = rest[:8], rest[8:]
    prev, rest = rest[:has_prev], rest[has_prev:]
    sums, w_out = rest[0], rest[1:9]
    tokg, cotg, upw, dnw, dnr, uterm, dterm, out_acc, in_acc = rest[9:]
    step = pl.program_id(0)
    per = acts.shape[2]
    many = tokg.shape[0]

    @pl.when(step == 0)
    def _():
        out_acc[...] = jnp.zeros_like(out_acc)
        in_acc[...] = jnp.zeros_like(in_acc)

    for b in range(many):
        j = base + step * many + b
        for at, ref, s in pieces(rows_tbl, w_in):
            upw[b, at, :] = ref[s, 0, b]
            dnr[b, at, :] = ref[s, 1, b]
        for k in range(KEEP):
            for which, kept, to in ((0, upk, tokg), (1, dnk, cotg)):
                f = kept[j, k]
                to[b, :, cols(k)] = acts[f // per, which, f % per]
            dnw[b, :, cols(k)] = dnr[b, cols(k), :]

    pre = [jnp.dot(tokg[b], upw[b], preferred_element_type=F32) for b in range(many)]
    grad_hidden = [
        lax.dot_general(cotg[b], dnw[b], NT, preferred_element_type=F32) for b in range(many)
    ]
    acted = [gelu_and_slope(p) for p in pre]
    hidden = [h.astype(BF16) for h, _ in acted]
    grad_pre = [(g * s).astype(BF16) for g, (_, s) in zip(grad_hidden, acted)]
    for b in range(many):
        j = base + step * many + b
        dt = lax.dot_general(hidden[b], cotg[b], TN, preferred_element_type=F32).astype(BF16)
        for k in range(KEEP):
            dterm[b, cols(k), :] = dt[:, cols(k)]
        uterm[b] = lax.dot_general(
            tokg[b], grad_pre[b], TN, preferred_element_type=F32).astype(BF16)
        for k in range(KEEP):
            out_acc[dnk[j, k]] += jnp.dot(hidden[b], dnr[b, cols(k), :], preferred_element_type=F32)
            in_acc[upk[j, k]] += lax.dot_general(
                grad_pre[b], upw[b, cols(k), :], NT, preferred_element_type=F32
            )
    for b in range(many):
        for at, ref, s in pieces(rows_tbl, w_out):
            ref[s, 0, b] = uterm[b, at, :]
            ref[s, 1, b] = dterm[b, at, :]

    @pl.when(step == pl.num_programs(0) - 1)
    def _():
        for s in range(sums.shape[0]):
            for which, acc in enumerate((out_acc, in_acc)):
                for i in range(per):
                    total = acc[s * per + i]
                    if has_prev:
                        total = total + prev[0][s, which, :, cols(i)].astype(F32)
                    sums[s, which, :, cols(i)] = total.astype(BF16)


def layer_part(base, rows_tbl, upk, dnk, acts, group, prev):
    local, part = group[0].shape[2:4]
    shards, _, per, tokens, _ = acts.shape
    many = MANY
    piece = pl.BlockSpec((2, 2, many, part, BLK), lambda j, *_: (0, 0, j, 0, 0))
    sums = jax.ShapeDtypeStruct((shards, 2, tokens, per * BLK), BF16)
    whole = pl.BlockSpec(sums.shape, lambda j, *_: (0,) * 4, pipeline_mode=pl.Buffered(1))
    term = jax.ShapeDtypeStruct(group[0].shape, BF16)
    extra = [] if prev is None else [prev]
    outs = pl.pallas_call(
        functools.partial(layer_kernel, base, len(extra)),
        grid_spec=pltpu.PrefetchScalarGridSpec(
            num_scalar_prefetch=3,
            grid=(local // many,),
            in_specs=[pl.BlockSpec(acts.shape, lambda j, *_: (0,) * 5, pipeline_mode=pl.Buffered(1))]
            + [piece] * 8 + [whole] * len(extra),
            out_specs=[whole] + [piece] * 8,
            scratch_shapes=[
                pltpu.VMEM((many, tokens, ROWS), BF16),
                pltpu.VMEM((many, tokens, ROWS), BF16),
                pltpu.VMEM((many, ROWS, BLK), BF16),
                pltpu.VMEM((many, BLK, ROWS), BF16),
                pltpu.VMEM((many, ROWS, BLK), BF16),
                pltpu.VMEM((many, ROWS, BLK), BF16),
                pltpu.VMEM((many, ROWS, BLK), BF16),
                pltpu.VMEM((NFB, tokens, BLK), F32),
                pltpu.VMEM((NFB, tokens, BLK), F32),
            ],
        ),
        out_shape=[sums] + [term] * 8,
        compiler_params=pltpu.CompilerParams(vmem_limit_bytes=VMEM_LIMIT),
        cost_estimate=pl.CostEstimate(
            flops=local * 24 * tokens * ROWS * BLK,
            bytes_accessed=4 * NFB * tokens * BLK * 2 + 8 * local * ROWS * BLK,
            transcendentals=local * tokens * BLK,
        ),
    )(rows_tbl, upk, dnk, acts, *group, *extra)
    return outs[0], outs[1:]


def shift(value, leg, by):
    pairs = []
    for y in range(SIDE):
        for x in range(SIDE):
            for t in range(TENSOR):
                along_x = t % 2 == leg
                to = (y, (x + by) % SIDE) if along_x else ((y + by) % SIDE, x)
                pairs.append(((y * SIDE + x) * TENSOR + t, (to[0] * SIDE + to[1]) * TENSOR + t))
    return lax.ppermute(value, ("dp", "tensor"), pairs)


def add(*terms):
    return sum(t.astype(F32) for t in terms).astype(BF16)


def near(shard):
    return shift(shard, 0, 1), shift(shard, 0, -1), shift(shard, 0, 2)


def cross(shard, got):
    a, b = jnp.stack([shard, got[0]]), jnp.stack([got[1], got[2]])
    return a, b, shift(a, 1, 1), shift(b, 1, 1), shift(a, 1, -1), shift(b, 1, -1)


def onward(group):
    return shift(group[2], 1, 1), shift(group[5], 1, -1)


def send_far(terms):
    _, _, to_minus_a, _, _, to_plus_b, far_a, far_b = terms
    return shift(far_a, 1, 1), shift(far_b, 1, -1), shift(to_plus_b, 1, 1), shift(to_minus_a, 1, -1)


def send_near(terms, got):
    to_minus_b, to_plus_a = terms[3], terms[4]
    return shift(add(to_plus_a, got[0]), 1, 1), shift(add(to_minus_b, got[1]), 1, -1)


def send_slots(terms, got, got_near):
    a, b = (terms[0], got_near[0], got[3]), (terms[1], got[2], got_near[1])
    slot = [add(*(p[s] for p in half)) for half in (a, b) for s in range(2)]
    return slot[0], shift(slot[1], 0, -1), shift(slot[2], 0, 1), shift(slot[3], 0, 2)


def tie(*values):
    return lax.optimization_barrier(values)


def body(tokens, cotangent, up_weight, down_weight, up_kept, down_kept):
    count, part = up_weight.shape[:2]
    rows = tokens.shape[0]
    shards = D // tokens.shape[1]

    def blocks(a):
        return a.reshape(rows, -1, BLK).transpose(1, 0, 2)

    acts = lax.all_gather(jnp.stack([blocks(tokens), blocks(cotangent)]), "tensor", axis=0)

    me = lax.axis_index("dp")
    y, x = me // SIDE, me % SIDE
    far = jnp.array(STEP, jnp.int32)
    ys, xs = (y + far) % SIDE, (x + far) % SIDE
    rows_tbl = part * jnp.where(
        lax.axis_index("tensor") % 2 == 0,
        ys[:, None] * SIDE + xs[None, :],
        ys[None, :] * SIDE + xs[:, None],
    ).reshape(-1)

    first = 6
    w = tuple(
        jnp.stack([up_weight[s], down_weight[s]]) for s in (slice(0, first), slice(first, count))
    )

    n0 = near(w[0])
    n0, w = tie(n0, w)

    c0 = cross(w[0], n0)
    c0, w = tie(c0, w)

    g0, n1 = c0 + onward(c0), near(w[1])
    g0, n1, acts = tie(g0, n1, acts)

    c1 = cross(w[1], n1)
    sums, t0 = layer_part(0, rows_tbl, up_kept, down_kept, acts, g0, None)
    c1, sums, t0, acts = tie(c1, sums, t0, acts)

    g1, f0 = c1 + onward(c1), send_far(t0)
    g1, sums, acts = tie(g1, sums, acts)

    sums, t1 = layer_part(first, rows_tbl, up_kept, down_kept, acts, g1, sums)
    sums, t0, t1, f0 = tie(sums, t0, t1, f0)

    summed = lax.psum_scatter(sums, "tensor", scatter_dimension=0)
    s0, f1 = send_near(t0, f0), send_far(t1)
    s0, f1 = tie(s0, f1)

    l0, s1 = send_slots(t0, f0, s0), send_near(t1, f1)
    l0, s1 = tie(l0, s1)

    l1 = send_slots(t1, f1, s1)
    ups, dns = zip(*(add(*part) for part in (l0, l1)))
    return summed[0], summed[1], jnp.concatenate(ups), jnp.concatenate(dns)


def solution(mesh):
    placed = (
        P("dp", "tensor"),
        P("dp", "tensor"),
        P("tensor", "dp", None),
        P("tensor", "dp", None),
        P("tensor", None),
        P("tensor", None),
    )
    return jax.shard_map(
        body,
        mesh=mesh,
        in_specs=placed,
        out_specs=placed[:4],
        check_vma=False,
    )
```

```python
import functools

import jax
import jax.numpy as jnp
from jax import lax
from jax.experimental import pallas as pl
from jax.experimental.pallas import tpu as pltpu
from jax.sharding import PartitionSpec as P

D = 7168
BLK = 128
KEEP = 14
NFB = D // BLK
ROWS = KEEP * BLK
F32 = jnp.float32
BF16 = jnp.bfloat16
SIDE = 4
STEP = (0, -1, 1, 2)
TENSOR = 8
VMEM_LIMIT = 56 * 2**20
MANY = 2
NT = (((1,), (1,)), ((), ()))
TN = (((0,), (0,)), ((), ()))


def gelu_and_slope(v):
    c = 0.7978845608028654
    v2 = v * v
    th = jnp.tanh(c * (v + 0.044715 * v * v2))
    half = 0.5 * (1.0 + th)
    slope = half + 0.5 * v * (1.0 - th * th) * (c * (1.0 + 3 * 0.044715 * v2))
    return v * half, slope


def cols(k):
    return slice(k * BLK, (k + 1) * BLK)


WHOLE = [[(g, s) for s in range(4)] for g in range(4)]
GATHERED = [g[n:n + 2] for g in WHOLE for n in (0, 2)]
SENT = [WHOLE[0], WHOLE[1][2:], WHOLE[2][:2], WHOLE[3][:2] + WHOLE[2][2:], WHOLE[1][:2] + WHOLE[3][2:]]


def pieces(rows_tbl, lists, refs):
    for ref, entries in zip(refs, lists):
        for n, (g, s) in enumerate(entries):
            yield pl.ds(pl.multiple_of(rows_tbl[g * 4 + s], 16), ref.shape[3]), ref, n


def layer_kernel(base, has_prev, rows_tbl, upk, dnk, acts_hbm, *rest):
    w_in, rest = rest[:8], rest[8:]
    prev, rest = rest[:has_prev], rest[has_prev:]
    sums_hbm, w_out = rest[0], rest[1:6]
    (tokg, cotg, upw, dnw, dnr, uterm, dterm, out_acc, in_acc,
     acts, sums, acts_sem, prev_sem, sums_sem) = rest[6:]
    step = pl.program_id(0)
    per = acts.shape[2]
    many = tokg.shape[0]
    acts_copy = pltpu.make_async_copy(acts_hbm, acts, acts_sem)

    @pl.when(step == 0)
    def _():
        acts_copy.start()
        if has_prev:
            pltpu.make_async_copy(prev[0], sums, prev_sem).start()
        def clear(f, carry):
            out_acc[f] = jnp.zeros(out_acc.shape[1:], F32)
            in_acc[f] = jnp.zeros(in_acc.shape[1:], F32)
            return carry

        lax.fori_loop(0, NFB, clear, 0)
        acts_copy.wait()

    for b in range(many):
        j = base + step * many + b
        for at, ref, s in pieces(rows_tbl, GATHERED, w_in):
            upw[b, at, :] = ref[s, 0, b]
            dnr[b, at, :] = ref[s, 1, b]
        for k in range(KEEP):
            for which, kept, to in ((0, upk, tokg), (1, dnk, cotg)):
                f = kept[j, k]
                to[b, :, cols(k)] = acts[f // per, which, f % per]
            dnw[b, :, cols(k)] = dnr[b, cols(k), :]

    pre = [jnp.dot(tokg[b], upw[b], preferred_element_type=F32) for b in range(many)]
    grad_hidden = [
        lax.dot_general(cotg[b], dnw[b], NT, preferred_element_type=F32) for b in range(many)
    ]
    acted = [gelu_and_slope(p) for p in pre]
    hidden = [h.astype(BF16) for h, _ in acted]
    grad_pre = [(g * s).astype(BF16) for g, (_, s) in zip(grad_hidden, acted)]
    for b in range(many):
        j = base + step * many + b
        dt = lax.dot_general(hidden[b], cotg[b], TN, preferred_element_type=F32).astype(BF16)
        for k in range(KEEP):
            dterm[b, cols(k), :] = dt[:, cols(k)]
        uterm[b] = lax.dot_general(
            tokg[b], grad_pre[b], TN, preferred_element_type=F32).astype(BF16)
        for k in range(KEEP):
            out_acc[dnk[j, k]] += jnp.dot(hidden[b], dnr[b, cols(k), :], preferred_element_type=F32)
            in_acc[upk[j, k]] += lax.dot_general(
                grad_pre[b], upw[b, cols(k), :], NT, preferred_element_type=F32
            )
    for b in range(many):
        for at, ref, s in pieces(rows_tbl, SENT, w_out):
            ref[s, 0, b] = uterm[b, at, :]
            ref[s, 1, b] = dterm[b, at, :]

    @pl.when(step == pl.num_programs(0) - 1)
    def _():
        if has_prev:
            pltpu.make_async_copy(prev[0], sums, prev_sem).wait()

        def copy_back(s):
            return pltpu.make_async_copy(sums.at[s], sums_hbm.at[s], sums_sem.at[s])

        def finish(s, carry):
            for which, acc in enumerate((out_acc, in_acc)):
                for i in range(per):
                    total = acc[s * per + i]
                    if has_prev:
                        total = total + sums[s, which, :, cols(i)].astype(F32)
                    sums[s, which, :, cols(i)] = total.astype(BF16)
            copy_back(s).start()
            return carry

        lax.fori_loop(0, sums.shape[0], finish, 0)
        for s in range(sums.shape[0]):
            copy_back(s).wait()


def layer_part(base, first, local, rows_tbl, upk, dnk, acts, group, prev):
    part = group[0].shape[3]
    shards, _, per, tokens, _ = acts.shape
    many = MANY
    skip = first // many

    def piece(entries, offset):
        return pl.BlockSpec((len(entries), 2, many, part, BLK), lambda j, *_: (0, 0, j + offset, 0, 0))

    anywhere = pl.BlockSpec(memory_space=pl.ANY)
    sums = jax.ShapeDtypeStruct((shards, 2, tokens, per * BLK), BF16)
    extra = [] if prev is None else [prev]
    outs = pl.pallas_call(
        functools.partial(layer_kernel, base + first, len(extra)),
        grid_spec=pltpu.PrefetchScalarGridSpec(
            num_scalar_prefetch=3,
            grid=(local // many,),
            in_specs=[anywhere] + [piece(e, skip) for e in GATHERED] + [anywhere] * len(extra),
            out_specs=[anywhere] + [piece(e, 0) for e in SENT],
            scratch_shapes=[
                pltpu.VMEM((many, tokens, ROWS), BF16),
                pltpu.VMEM((many, tokens, ROWS), BF16),
                pltpu.VMEM((many, ROWS, BLK), BF16),
                pltpu.VMEM((many, BLK, ROWS), BF16),
                pltpu.VMEM((many, ROWS, BLK), BF16),
                pltpu.VMEM((many, ROWS, BLK), BF16),
                pltpu.VMEM((many, ROWS, BLK), BF16),
                pltpu.VMEM((NFB, tokens, BLK), F32),
                pltpu.VMEM((NFB, tokens, BLK), F32),
                pltpu.VMEM(acts.shape, BF16),
                pltpu.VMEM(sums.shape, BF16),
                pltpu.SemaphoreType.DMA,
                pltpu.SemaphoreType.DMA,
                pltpu.SemaphoreType.DMA((shards,)),
            ],
        ),
        out_shape=[sums] + [
            jax.ShapeDtypeStruct((len(e), 2, local, part, BLK), BF16) for e in SENT],
        compiler_params=pltpu.CompilerParams(vmem_limit_bytes=VMEM_LIMIT),
        cost_estimate=pl.CostEstimate(
            flops=local * 24 * tokens * ROWS * BLK,
            bytes_accessed=4 * NFB * tokens * BLK * 2 + 8 * local * ROWS * BLK,
            transcendentals=local * tokens * BLK,
        ),
    )(rows_tbl, upk, dnk, acts, *group, *extra)
    return outs[0], outs[1:]


def pack_kernel(tokens, cotangent, out):
    for which, ref in enumerate((tokens, cotangent)):
        for i in range(out.shape[1]):
            out[which, i] = ref[:, cols(i)]


def pack(tokens, cotangent):
    rows, width = tokens.shape
    return pl.pallas_call(
        pack_kernel,
        out_shape=jax.ShapeDtypeStruct((2, width // BLK, rows, BLK), BF16),
    )(tokens, cotangent)


def shift(value, leg, by):
    pairs = []
    for y in range(SIDE):
        for x in range(SIDE):
            for t in range(TENSOR):
                along_x = t % 2 == leg
                to = (y, (x + by) % SIDE) if along_x else ((y + by) % SIDE, x)
                pairs.append(((y * SIDE + x) * TENSOR + t, (to[0] * SIDE + to[1]) * TENSOR + t))
    return lax.ppermute(value, ("dp", "tensor"), pairs)


def add(*terms):
    return sum(t.astype(F32) for t in terms).astype(BF16)


def near(shard):
    return shift(shard, 0, 1), shift(shard, 0, -1), shift(shard, 0, 2)


def cross(shard, got):
    a, b = jnp.stack([shard, got[0]]), jnp.stack([got[1], got[2]])
    return a, b, shift(a, 1, 1), shift(b, 1, 1), shift(a, 1, -1), shift(b, 1, -1)


def onward(group):
    return shift(group[2], 1, 1), shift(group[5], 1, -1)


def send_far(terms):
    return shift(terms[3], 1, 1), shift(terms[4], 1, -1)


def send_near(terms, got):
    return shift(add(terms[2], got[0][:2]), 1, 1), shift(add(terms[1], got[1][2:]), 1, -1)


def send_slots(terms, got, got_near):
    slot = [add(terms[0][s], got_near[0][s], got[1][s]) for s in (0, 1)]
    slot += [add(terms[0][s], got_near[1][s - 2], got[0][s]) for s in (2, 3)]
    return slot[0], shift(slot[1], 0, -1), shift(slot[2], 0, 1), shift(slot[3], 0, 2)


def tie(*values):
    return lax.optimization_barrier(values)


def body(tokens, cotangent, up_weight, down_weight, up_kept, down_kept):
    count, part = up_weight.shape[:2]

    acts = lax.all_gather(pack(tokens, cotangent), "tensor", axis=0)

    me = lax.axis_index("dp")
    y, x = me // SIDE, me % SIDE
    far = jnp.array(STEP, jnp.int32)
    ys, xs = (y + far) % SIDE, (x + far) % SIDE
    rows_tbl = part * jnp.where(
        lax.axis_index("tensor") % 2 == 0,
        ys[:, None] * SIDE + xs[None, :],
        ys[None, :] * SIDE + xs[:, None],
    ).reshape(-1)

    first = 6
    mid = (count - first) // 2
    w = tuple(
        jnp.stack([up_weight[s], down_weight[s]]) for s in (slice(0, first), slice(first, count))
    )

    n0 = near(w[0])
    n0, w = tie(n0, w)

    c0 = cross(w[0], n0)
    c0, w = tie(c0, w)

    g0, n1 = c0 + onward(c0), near(w[1])
    g0, n1, acts = tie(g0, n1, acts)

    c1 = cross(w[1], n1)
    sums, t0 = layer_part(0, 0, first, rows_tbl, up_kept, down_kept, acts, g0, None)
    c1, sums, t0, acts = tie(c1, sums, t0, acts)

    g1, f0 = c1 + onward(c1), send_far(t0)
    g1, sums, acts = tie(g1, sums, acts)

    sums, t1 = layer_part(first, 0, mid, rows_tbl, up_kept, down_kept, acts, g1, sums)
    sums, t0, t1, f0, g1, acts = tie(sums, t0, t1, f0, g1, acts)

    s0, f1 = send_near(t0, f0), send_far(t1)
    sums, t2 = layer_part(first, mid, mid, rows_tbl, up_kept, down_kept, acts, g1, sums)
    sums, t0, t1, t2, f0, f1, s0 = tie(sums, t0, t1, t2, f0, f1, s0)

    summed = lax.psum_scatter(sums, "tensor", scatter_dimension=0)
    s1, f2, l0 = send_near(t1, f1), send_far(t2), send_slots(t0, f0, s0)
    s1, f2, l0 = tie(s1, f2, l0)

    s2, l1 = send_near(t2, f2), send_slots(t1, f1, s1)
    s2, l1 = tie(s2, l1)

    l2 = send_slots(t2, f2, s2)
    summed, l2 = tie((summed[0], summed[1]), l2)
    ups, dns = zip(*(add(*part) for part in (l0, l1, l2)))
    return summed[0], summed[1], jnp.concatenate(ups), jnp.concatenate(dns)


def solution(mesh):
    placed = (
        P("dp", "tensor"),
        P("dp", "tensor"),
        P("tensor", "dp", None),
        P("tensor", "dp", None),
        P("tensor", None),
        P("tensor", None),
    )
    return jax.shard_map(
        body,
        mesh=mesh,
        in_specs=placed,
        out_specs=placed[:4],
        check_vma=False,
    )
```

```python
import functools

import jax
import jax.numpy as jnp
from jax import lax
from jax.experimental import pallas as pl
from jax.experimental.pallas import tpu as pltpu
from jax.sharding import PartitionSpec as P

D = 7168
BLK = 128
KEEP = 14
NFB = D // BLK
ROWS = KEEP * BLK
F32 = jnp.float32
BF16 = jnp.bfloat16
SIDE = 4
STEP = (0, -1, 1, 2)
TENSOR = 8
VMEM_LIMIT = 56 * 2**20
MANY = 2
NT = (((1,), (1,)), ((), ()))
TN = (((0,), (0,)), ((), ()))


def gelu_and_slope(v):
    c = 0.7978845608028654
    v2 = v * v
    th = jnp.tanh(c * (v + 0.044715 * v * v2))
    half = 0.5 * (1.0 + th)
    slope = half + 0.5 * v * (1.0 - th * th) * (c * (1.0 + 3 * 0.044715 * v2))
    return v * half, slope


def cols(k):
    return slice(k * BLK, (k + 1) * BLK)


WHOLE = [[(g, s) for s in range(4)] for g in range(4)]
GATHERED = [g[n:n + 2] for g in WHOLE for n in (0, 2)]
SENT = [WHOLE[0], WHOLE[1][2:], WHOLE[2][:2], WHOLE[3][:2] + WHOLE[2][2:], WHOLE[1][:2] + WHOLE[3][2:]]


def pieces(rows_tbl, lists, refs):
    for ref, entries in zip(refs, lists):
        for n, (g, s) in enumerate(entries):
            yield pl.ds(pl.multiple_of(rows_tbl[g * 4 + s], 16), ref.shape[3]), ref, n


def layer_kernel(base, has_prev, rows_tbl, upk, dnk, acts_hbm, *rest):
    w_in, rest = rest[:8], rest[8:]
    prev, rest = rest[:has_prev], rest[has_prev:]
    sums_hbm, w_out = rest[0], rest[1:6]
    (tokg, cotg, upw, dnw, dnr, uterm, dterm, out_acc, in_acc,
     acts, sums, acts_sem, prev_sem, sums_sem) = rest[6:]
    step = pl.program_id(0)
    per = acts.shape[2]
    many = tokg.shape[0]
    acts_copy = pltpu.make_async_copy(acts_hbm, acts, acts_sem)

    @pl.when(step == 0)
    def _():
        acts_copy.start()
        if has_prev:
            pltpu.make_async_copy(prev[0], sums, prev_sem).start()
        def clear(f, carry):
            out_acc[f] = jnp.zeros(out_acc.shape[1:], F32)
            in_acc[f] = jnp.zeros(in_acc.shape[1:], F32)
            return carry

        lax.fori_loop(0, NFB, clear, 0)
        acts_copy.wait()

    for b in range(many):
        j = base + step * many + b
        for at, ref, s in pieces(rows_tbl, GATHERED, w_in):
            upw[b, at, :] = ref[s, 0, b]
            dnr[b, at, :] = ref[s, 1, b]
        for k in range(KEEP):
            for which, kept, to in ((0, upk, tokg), (1, dnk, cotg)):
                f = kept[j, k]
                to[b, :, cols(k)] = acts[f // per, which, f % per]
            dnw[b, :, cols(k)] = dnr[b, cols(k), :]

    pre = [jnp.dot(tokg[b], upw[b], preferred_element_type=F32) for b in range(many)]
    grad_hidden = [
        lax.dot_general(cotg[b], dnw[b], NT, preferred_element_type=F32) for b in range(many)
    ]
    acted = [gelu_and_slope(p) for p in pre]
    hidden = [h.astype(BF16) for h, _ in acted]
    grad_pre = [(g * s).astype(BF16) for g, (_, s) in zip(grad_hidden, acted)]
    for b in range(many):
        j = base + step * many + b
        dt = lax.dot_general(hidden[b], cotg[b], TN, preferred_element_type=F32).astype(BF16)
        for k in range(KEEP):
            dterm[b, cols(k), :] = dt[:, cols(k)]
        uterm[b] = lax.dot_general(
            tokg[b], grad_pre[b], TN, preferred_element_type=F32).astype(BF16)
        for k in range(KEEP):
            out_acc[dnk[j, k]] += jnp.dot(hidden[b], dnr[b, cols(k), :], preferred_element_type=F32)
            in_acc[upk[j, k]] += lax.dot_general(
                grad_pre[b], upw[b, cols(k), :], NT, preferred_element_type=F32
            )
    for b in range(many):
        for at, ref, s in pieces(rows_tbl, SENT, w_out):
            ref[s, 0, b] = uterm[b, at, :]
            ref[s, 1, b] = dterm[b, at, :]

    @pl.when(step == pl.num_programs(0) - 1)
    def _():
        if has_prev:
            pltpu.make_async_copy(prev[0], sums, prev_sem).wait()

        def copy_back(s):
            return pltpu.make_async_copy(sums.at[s], sums_hbm.at[s], sums_sem.at[s])

        def finish(s, carry):
            for which, acc in enumerate((out_acc, in_acc)):
                for i in range(per):
                    total = acc[s * per + i]
                    if has_prev:
                        total = total + sums[s, which, :, cols(i)].astype(F32)
                    sums[s, which, :, cols(i)] = total.astype(BF16)
            copy_back(s).start()
            return carry

        lax.fori_loop(0, sums.shape[0], finish, 0)
        for s in range(sums.shape[0]):
            copy_back(s).wait()


def layer_part(base, first, local, rows_tbl, upk, dnk, acts, group, prev):
    part = group[0].shape[3]
    shards, _, per, tokens, _ = acts.shape
    many = MANY
    skip = first // many

    def piece(entries, offset):
        return pl.BlockSpec((len(entries), 2, many, part, BLK), lambda j, *_: (0, 0, j + offset, 0, 0))

    anywhere = pl.BlockSpec(memory_space=pl.ANY)
    sums = jax.ShapeDtypeStruct((shards, 2, tokens, per * BLK), BF16)
    extra = [] if prev is None else [prev]
    outs = pl.pallas_call(
        functools.partial(layer_kernel, base + first, len(extra)),
        grid_spec=pltpu.PrefetchScalarGridSpec(
            num_scalar_prefetch=3,
            grid=(local // many,),
            in_specs=[anywhere] + [piece(e, skip) for e in GATHERED] + [anywhere] * len(extra),
            out_specs=[anywhere] + [piece(e, 0) for e in SENT],
            scratch_shapes=[
                pltpu.VMEM((many, tokens, ROWS), BF16),
                pltpu.VMEM((many, tokens, ROWS), BF16),
                pltpu.VMEM((many, ROWS, BLK), BF16),
                pltpu.VMEM((many, BLK, ROWS), BF16),
                pltpu.VMEM((many, ROWS, BLK), BF16),
                pltpu.VMEM((many, ROWS, BLK), BF16),
                pltpu.VMEM((many, ROWS, BLK), BF16),
                pltpu.VMEM((NFB, tokens, BLK), F32),
                pltpu.VMEM((NFB, tokens, BLK), F32),
                pltpu.VMEM(acts.shape, BF16),
                pltpu.VMEM(sums.shape, BF16),
                pltpu.SemaphoreType.DMA,
                pltpu.SemaphoreType.DMA,
                pltpu.SemaphoreType.DMA((shards,)),
            ],
        ),
        out_shape=[sums] + [
            jax.ShapeDtypeStruct((len(e), 2, local, part, BLK), BF16) for e in SENT],
        compiler_params=pltpu.CompilerParams(vmem_limit_bytes=VMEM_LIMIT),
        cost_estimate=pl.CostEstimate(
            flops=local * 24 * tokens * ROWS * BLK,
            bytes_accessed=4 * NFB * tokens * BLK * 2 + 8 * local * ROWS * BLK,
            transcendentals=local * tokens * BLK,
        ),
    )(rows_tbl, upk, dnk, acts, *group, *extra)
    return outs[0], outs[1:]


def pack_kernel(tokens, cotangent, out):
    for which, ref in enumerate((tokens, cotangent)):
        for i in range(out.shape[1]):
            out[which, i] = ref[:, cols(i)]


def pack(tokens, cotangent):
    rows, width = tokens.shape
    return pl.pallas_call(
        pack_kernel,
        out_shape=jax.ShapeDtypeStruct((2, width // BLK, rows, BLK), BF16),
    )(tokens, cotangent)


def shift(value, leg, by):
    pairs = []
    for y in range(SIDE):
        for x in range(SIDE):
            for t in range(TENSOR):
                along_x = t % 2 == leg
                to = (y, (x + by) % SIDE) if along_x else ((y + by) % SIDE, x)
                pairs.append(((y * SIDE + x) * TENSOR + t, (to[0] * SIDE + to[1]) * TENSOR + t))
    return lax.ppermute(value, ("dp", "tensor"), pairs)


def add(*terms):
    return sum(t.astype(F32) for t in terms).astype(BF16)


def near(shard):
    return shift(shard, 0, 1), shift(shard, 0, -1), shift(shard, 0, 2)


def cross(shard, got):
    a, b = jnp.stack([shard, got[0]]), jnp.stack([got[1], got[2]])
    return a, b, shift(a, 1, 1), shift(b, 1, 1), shift(a, 1, -1), shift(b, 1, -1)


def onward(group):
    return shift(group[2], 1, 1), shift(group[5], 1, -1)


def send_far(terms):
    return shift(terms[3], 1, 1), shift(terms[4], 1, -1)


def send_near(terms, got):
    return shift(add(terms[2], got[0][:2]), 1, 1), shift(add(terms[1], got[1][2:]), 1, -1)


def send_slots(terms, got, got_near):
    slot = [add(terms[0][s], got_near[0][s], got[1][s]) for s in (0, 1)]
    slot += [add(terms[0][s], got_near[1][s - 2], got[0][s]) for s in (2, 3)]
    return slot[0], shift(slot[1], 0, -1), shift(slot[2], 0, 1), shift(slot[3], 0, 2)


def tie(*values):
    return lax.optimization_barrier(values)


def body(tokens, cotangent, up_weight, down_weight, up_kept, down_kept):
    count, part = up_weight.shape[:2]

    acts = lax.all_gather(pack(tokens, cotangent), "tensor", axis=0)

    me = lax.axis_index("dp")
    y, x = me // SIDE, me % SIDE
    far = jnp.array(STEP, jnp.int32)
    ys, xs = (y + far) % SIDE, (x + far) % SIDE
    rows_tbl = part * jnp.where(
        lax.axis_index("tensor") % 2 == 0,
        ys[:, None] * SIDE + xs[None, :],
        ys[None, :] * SIDE + xs[:, None],
    ).reshape(-1)

    first = 6
    mid = (count - first) // 2
    w = tuple(
        jnp.stack([up_weight[s], down_weight[s]]) for s in (slice(0, first), slice(first, count))
    )

    n0 = near(w[0])
    c0 = cross(w[0], n0)
    c0, w = tie(c0, w)

    g0, n1 = c0 + onward(c0), near(w[1])
    g0, n1, acts = tie(g0, n1, acts)

    c1 = cross(w[1], n1)
    sums, t0 = layer_part(0, 0, first, rows_tbl, up_kept, down_kept, acts, g0, None)
    c1, sums, t0, acts = tie(c1, sums, t0, acts)

    g1, f0 = c1 + onward(c1), send_far(t0)
    g1, sums, acts = tie(g1, sums, acts)

    sums, t1 = layer_part(first, 0, mid, rows_tbl, up_kept, down_kept, acts, g1, sums)
    sums, t0, t1, f0, g1, acts = tie(sums, t0, t1, f0, g1, acts)

    s0, f1 = send_near(t0, f0), send_far(t1)
    sums, t2 = layer_part(first, mid, mid, rows_tbl, up_kept, down_kept, acts, g1, sums)
    sums, t0, t1, t2, f0, f1, s0 = tie(sums, t0, t1, t2, f0, f1, s0)

    summed = lax.psum_scatter(sums, "tensor", scatter_dimension=0)
    s1, f2, l0 = send_near(t1, f1), send_far(t2), send_slots(t0, f0, s0)
    s1, f2, l0 = tie(s1, f2, l0)

    s2, l1 = send_near(t2, f2), send_slots(t1, f1, s1)
    s2, l1 = tie(s2, l1)

    l2 = send_slots(t2, f2, s2)
    summed, l2 = tie((summed[0], summed[1]), l2)
    ups, dns = zip(*(add(*part) for part in (l0, l1, l2)))
    return summed[0], summed[1], jnp.concatenate(ups), jnp.concatenate(dns)


def solution(mesh):
    placed = (
        P("dp", "tensor"),
        P("dp", "tensor"),
        P("tensor", "dp", None),
        P("tensor", "dp", None),
        P("tensor", None),
        P("tensor", None),
    )
    return jax.shard_map(
        body,
        mesh=mesh,
        in_specs=placed,
        out_specs=placed[:4],
        check_vma=False,
    )
```
